32 devices in a mesh: section: 4 (over y, x), dp: 8 (over z, core).
Axes of the slice: x: 2, y: 2, z: 4, core: 2. Of those that a mesh axis runs over, the one named last changes fastest.
Arguments:
- frozen: bfloat16 [4, 8192, 8192], P('section', 'dp'), may hold values from -0.0625 to 0.0625
- adapt_down: bfloat16 [4, 16, 8192, 64], P('section', 'dp'), may hold values from -0.0625 to 0.0625
- adapt_up: bfloat16 [4, 16, 64, 8192], P('section', 'dp'), may hold values from -0.0625 to 0.0625
- saved_inputs: bfloat16 [4, 1, 24, 8192], P('section', None, None, 'dp'), may hold values from -6 to 6
- out_grad: bfloat16 [1, 24, 8192], P(None, None, 'dp'), may hold values from -6 to 6
- sensor: int32 [1, 8], replicated, may hold values from 0 to 15, as said below
- counts: int32 [16], P('dp'), may hold values from 256 to 2047
Outputs:
- in_grad: bfloat16 [4, 1, 24, 8192], P('section', None, None, 'dp')
- grad_down: bfloat16 [4, 16, 8192, 64], P('section', 'dp')
- grad_up: bfloat16 [4, 16, 64, 8192], P('section', 'dp')
The draws below stay inside these ranges and needn't reach their ends.
Inputs may be any that keep to these rules, and one draw needn't show every extreme that they name: `sensor`: in each micro-batch at most 2 blocks have sensors s with s // 2 equal to one given value, and exactly 2 for some value.
All inputs are finite; a program needn't handle non-finite values.
Results may differ from the reference program's by a relative error of at most 0.013.
Values may be sent and summed in bfloat16 or wider, within the bound.
A program may use at most 128 MiB of HBM per device.

```python
import math
import jax
import jax.numpy as jnp
from jax import lax

D = 8192
R = 64
BLK = 3
SEN_DEV = 2
CAP = 2
MB = 1
SECTIONS = 4
BLOCKS = 8
TOKS = 24
SENSORS = 16


def draw_sensor(key, part):
    keys = jax.random.split(jax.random.fold_in(key, 17), MB)

    def single(sub):
        first, second, third, fourth = jax.random.split(sub, 4)
        hot = jax.random.randint(first, (), 0, BLOCKS).astype(jnp.int32)
        total_pool = (BLOCKS - 1) * CAP
        pool = jnp.arange(total_pool, dtype=jnp.int32) // CAP
        pool = jnp.where(pool >= hot, pool + 1, pool)
        pool = jax.random.permutation(second, pool)
        ranks = jnp.arange(total_pool, dtype=jnp.int32)
        edge = (pool == 0) | (pool == BLOCKS - 1)
        score = ranks + jnp.where(edge, -total_pool, 0).astype(jnp.int32)
        order = jnp.argsort(score, stable=True)
        pool = pool[order][:BLOCKS - CAP]
        owners = jnp.concatenate([jnp.full((CAP,), hot, jnp.int32), pool])
        owners = jax.random.permutation(third, owners)
        local = jax.random.randint(fourth, (BLOCKS,), 0, SEN_DEV).astype(jnp.int32)
        top_mask = (owners == BLOCKS - 1).astype(jnp.int32)
        top_first = (top_mask == 1) & (jnp.cumsum(top_mask) == 1)
        low_mask = (owners == 0).astype(jnp.int32)
        low_first = (low_mask == 1) & (jnp.cumsum(low_mask) == 1)
        local = jnp.where(top_first, SEN_DEV - 1, local)
        local = jnp.where(low_first, 0, local)
        return (owners * SEN_DEV + local).astype(jnp.int32)
    return lax.map(single, keys)


def place_ends(values, own_key, least, top_value):
    index_at = [jax.random.randint(jax.random.fold_in(own_key, axis), (), 0, length) for axis, length in enumerate(values.shape)]
    main_axis = values.shape.index(max(values.shape))
    beside = index_at[:main_axis] + [(index_at[main_axis] + 1) % values.shape[main_axis]] + index_at[main_axis + 1:]
    return values.at[tuple(index_at)].set(least).at[tuple(beside)].set(top_value)


def block_levels(own_key, extent, shards, smallest, high):
    factor_of = 1.0
    for axis_at, parts in shards:
        heights = jax.random.uniform(jax.random.fold_in(jax.random.fold_in(own_key, 6), axis_at), (parts,), jnp.float32, smallest / len(shards), high / len(shards))
        factor_of = factor_of * jnp.repeat(jnp.exp(heights), extent[axis_at] // parts).reshape((-1,) + (1,) * (len(extent) - 1 - axis_at))
    return factor_of


def noise(stream_key, dims, scale, most, shards=(), kind=jnp.bfloat16):
    values = jax.random.normal(stream_key, dims, jnp.float32) * scale
    if len(shards) > 0:
        values = block_levels(stream_key, dims, shards, -0.22, 0.18) * values
    return jnp.clip(values, min=-most, max=most).astype(kind)


def setup_inputs(seed: int = 0) -> dict:
    streams_of = jax.random.split(jax.random.key(seed), 8)
    return {
        "frozen": noise(streams_of[0], (SECTIONS, D, D), D ** -0.5, 0.0625, ((0, 4), (1, 8))),
        "adapt_down": noise(streams_of[1], (SECTIONS, SENSORS, D, R), D ** -0.5, 0.0625, ((0, 4), (1, 8))),
        "adapt_up": noise(streams_of[2], (SECTIONS, SENSORS, R, D), D ** -0.5, 0.0625, ((0, 4), (1, 8))),
        "saved_inputs": noise(streams_of[3], (SECTIONS, MB, TOKS, D), 1.0, 6.0, ((0, 4), (3, 8))),
        "out_grad": noise(streams_of[4], (MB, TOKS, D), 1.0, 6.0, ((2, 8),)),
        "sensor": draw_sensor(jax.random.fold_in(streams_of[7], 71), 0),
        "counts": place_ends(jax.random.randint(streams_of[6], (SENSORS,), 256, 2048), jax.random.fold_in(streams_of[6], 1), 256, 2047).astype(jnp.int32),
    }


SCALE = 2.0
NORM_TOK = 1024.0
CLIP_RMS = 0.5

def reference(frozen, adapt_down, adapt_up, saved_inputs, out_grad, sensor, counts):
    current = out_grad
    grads_in = [None] * SECTIONS
    downs = [None] * SECTIONS
    ups = [None] * SECTIONS
    for section in reversed(range(SECTIONS)):
        weight = frozen[section]
        down_all = adapt_down[section]
        up_all = adapt_up[section]
        acc_down = jnp.zeros((SENSORS, D, R), jnp.float32)
        acc_up = jnp.zeros((SENSORS, R, D), jnp.float32)
        produced = []
        for micro in range(MB):
            grad = current[micro]
            inputs = saved_inputs[section, micro]
            frozen_part = jnp.dot(grad, weight.T, preferred_element_type=jnp.float32)

            def per_block(carry, item):
                acc_d, acc_u = carry
                grad_blk, input_blk, ident = item
                down_map = down_all[ident]
                up_map = up_all[ident]
                lowu = jnp.dot(grad_blk, up_map.T, preferred_element_type=jnp.float32).astype(jnp.bfloat16)
                lowv = jnp.dot(input_blk, down_map, preferred_element_type=jnp.float32).astype(jnp.bfloat16)
                term = (SCALE * jnp.dot(lowu, down_map.T, preferred_element_type=jnp.float32)).astype(jnp.bfloat16)
                acc_d = acc_d.at[ident].add(SCALE * jnp.dot(input_blk.T, lowu, preferred_element_type=jnp.float32))
                acc_u = acc_u.at[ident].add(SCALE * jnp.dot(lowv.T, grad_blk, preferred_element_type=jnp.float32))
                return ((acc_d, acc_u), term)
            (acc_down, acc_up), terms = lax.scan(per_block, (acc_down, acc_up), (grad.reshape(BLOCKS, BLK, D), inputs.reshape(BLOCKS, BLK, D), sensor[micro].astype(jnp.int32)))
            total_grad = (frozen_part + terms.reshape(TOKS, D).astype(jnp.float32)).astype(jnp.bfloat16)
            produced.append(total_grad)
        current = jnp.stack(produced)
        grads_in[section] = current
        downs[section] = acc_down
        ups[section] = acc_up
    weights = NORM_TOK / counts.astype(jnp.float32)
    scaled_down = jnp.stack(downs) * weights[None, :, None, None]
    scaled_up = jnp.stack(ups) * weights[None, :, None, None]
    total = jnp.sum(scaled_down * scaled_down) + jnp.sum(scaled_up * scaled_up)
    limit = CLIP_RMS * math.sqrt(2.0 * SECTIONS * SENSORS * D * R)
    factor = jnp.minimum(1.0, limit / jnp.sqrt(total + 1e-06))
    return (jnp.stack(grads_in), (scaled_down * factor).astype(jnp.bfloat16), (scaled_up * factor).astype(jnp.bfloat16))
```

```python
import functools
import math

import jax
import jax.numpy as jnp
from jax import lax
from jax.experimental import pallas as pl
from jax.experimental.pallas import tpu as pltpu
from jax.sharding import PartitionSpec as P

CAP = 2
SCALE = 2.0
NORM_TOK = 1024.0
CLIP_RMS = 0.5
MESH = pl.DeviceIdType.MESH
SLOT = 16


def mm_t(a, b):
    return lax.dot_general(a, b, (((1,), (1,)), ((), ())), preferred_element_type=jnp.float32)


def mm(a, b):
    return jnp.dot(a, b, preferred_element_type=jnp.float32)


def chain_kernel(
    n_sec, n_dp, rank, pack, limit,
    w_hbm, dn_hbm, up_hbm, x_in, g_in, sens_col, tgt_col, tgt_row, w2_col,
    res_out, x_out, g_out, u_out, v_out, fac_out,
    wbuf, dbuf, ubuf, xbuf, gbuf, lsend, lrecv, acc, uacc, vacc, gram_x, chain_in, chain_out, norms,
    w_sem, a_sem, o_sem, x_rs, x_ss, x_fs, g_rs, og_ss, g_ss, g_fs, l_ss, l_rs, c_ss, c_rs, n_ss, n_rs,
):
    sec = lax.axis_index("section")
    me = lax.axis_index("dp")
    par = lax.rem(me, 2)
    partner = me + 1 - 2 * par
    half = n_dp // 2
    my = me // 2
    way = 1 - 2 * (my // max(half // 2, 1))
    top = n_sec - 1
    is_top = sec == top
    tokens, columns = x_in.shape
    rows = xbuf.shape[1]
    wide = columns // pack
    lanes = uacc.shape[1]

    def near(k):
        return lax.rem(my + way * k + half, half)

    def cols(j):
        return pl.ds(pl.multiple_of(j * columns, columns), columns)

    def w_copy(j):
        return pltpu.make_async_copy(w_hbm.at[:, cols(j)], wbuf.at[:, cols(j)], w_sem.at[j])

    up_copy = pltpu.make_async_copy(up_hbm, ubuf, a_sem.at[0])
    dn_copy = pltpu.make_async_copy(dn_hbm, dbuf, a_sem.at[1])
    up_copy.start()
    dn_copy.start()

    def start_w(k, carry):
        w_copy(2 * near(k) + par).start()
        return carry

    def start_w_other(k, carry):
        w_copy(2 * near(k) + 1 - par).start()
        return carry

    lax.fori_loop(0, half, start_w, 0)
    lax.fori_loop(0, half, start_w_other, 0)

    barrier = pltpu.get_barrier_semaphore()
    for q in range(n_sec):
        def greet(d, carry, q=q):
            @pl.when((sec != q) | (me != d))
            def _():
                pl.semaphore_signal(barrier, inc=1, device_id=(q, d), device_id_type=MESH)
            return carry
        lax.fori_loop(0, n_dp, greet, 0)

    def padded(ref):
        value = ref[...]
        if rows == tokens:
            return value
        tail = jnp.zeros((rows - tokens, columns), jnp.float32)
        return jnp.concatenate([value.astype(jnp.float32), tail], axis=0).astype(jnp.bfloat16)

    xbuf[me] = padded(x_in)

    @pl.when(is_top)
    def _():
        gbuf[me] = padded(g_in)

    pl.semaphore_wait(barrier, n_sec * n_dp - 1)

    def remote(src, dst, ss, rs, q, d):
        return pltpu.make_async_remote_copy(
            src_ref=src, dst_ref=dst, send_sem=ss, recv_sem=rs, device_id=(q, d), device_id_type=MESH
        )

    def og_copy(k):
        return remote(gbuf.at[me], gbuf.at[me], og_ss.at[k], g_rs.at[me], sec, 2 * near(k) + par)

    def x_copy(k):
        return remote(xbuf.at[me], xbuf.at[me], x_ss.at[k], x_rs.at[me], sec, 2 * near(k) + par)

    def x_forward(j):
        return remote(xbuf.at[j], xbuf.at[j], x_fs.at[j // 2], x_rs.at[j], sec, partner)

    def g_forward(j):
        return remote(gbuf.at[j], gbuf.at[j], g_fs.at[j // 2], g_rs.at[j], sec, partner)

    def res_copy(k):
        return remote(res_out, gbuf.at[me], g_ss.at[k], g_rs.at[me], sec - 1, 2 * near(k) + par)

    def low_copy(j):
        return remote(lsend.at[j], lrecv.at[me], l_ss.at[j], l_rs.at[me], sec, j)

    def low_arrival(j):
        return remote(lsend.at[j], lrecv.at[j], l_ss.at[j], l_rs.at[j], sec, partner)

    def loop(lo, hi, body):
        def step(k, carry):
            body(k)
            return carry
        lax.fori_loop(lo, hi, step, 0)

    lane_sensor = lax.broadcasted_iota(jnp.int32, (rows, lanes), 1) // rank
    own = sens_col[...] == me * (lanes // rank) + lane_sensor

    def x_work():
        loop(1, half, lambda k: x_copy(k).start())
        vacc[...] = jnp.zeros_like(vacc)
        gram_x[...] = jnp.zeros_like(gram_x)

        def use(j):
            piece = xbuf[j]
            vacc[...] += mm_t(piece, dbuf[:, cols(j)])
            gram_x[...] += mm_t(piece, piece)

        def first(k):
            j = 2 * near(k) + par

            @pl.when(k > 0)
            def _():
                x_forward(j).wait_recv()
            x_forward(j).start()
            use(j)

        def second(k):
            j = 2 * near(k) + 1 - par
            x_forward(j).wait_recv()
            use(j)

        loop(0, half, first)
        loop(0, half, second)
        v_out[...] = jnp.where(own, vacc[...], 0.0).astype(jnp.bfloat16)
        pltpu.make_async_copy(xbuf, x_out, o_sem.at[0]).start()

    @pl.when(is_top)
    def _():
        loop(1, half, lambda k: og_copy(k).start())

    dn_copy.wait()
    up_copy.wait()

    @pl.when(sec != top)
    def _():
        x_work()

    acc[...] = jnp.zeros_like(acc)
    uacc[...] = jnp.zeros_like(uacc)

    def g_first(k):
        j = 2 * near(k) + par

        @pl.when((k > 0) | (sec != top))
        def _():
            g_forward(j).wait_recv()
        g_forward(j).start()
        w_copy(j).wait()
        piece = gbuf[j]
        uacc[...] += mm_t(piece, ubuf[:, cols(j)])
        acc[...] += mm_t(piece, wbuf[:, cols(j)])

    def g_second(k):
        j = 2 * near(k) + 1 - par
        g_forward(j).wait_recv()
        uacc[...] += mm_t(gbuf[j], ubuf[:, cols(j)])

    loop(0, half, g_first)
    loop(0, half, g_second)
    u_out[...] = jnp.where(own, uacc[...], 0.0).astype(jnp.bfloat16)

    slot_at = lax.broadcasted_iota(jnp.int32, (SLOT, rows), 0) + me * SLOT
    in_slot = lax.broadcasted_iota(jnp.int32, (SLOT, rows), 0) < SLOT // pack
    select = jnp.where((tgt_row[...] == slot_at) & in_slot, 1.0, 0.0).astype(jnp.bfloat16)
    u_sel = mm(select, u_out[...]).astype(jnp.bfloat16)

    def low_work(k):
        j = lax.rem(me + k, n_dp)
        low = SCALE * mm(u_sel, dbuf[:, cols(j)])
        if pack == 2:
            low = jnp.concatenate([low[: SLOT // 2, :wide], low[: SLOT // 2, wide:]], axis=0)
        low = low.astype(jnp.bfloat16)

        @pl.when(k < n_dp)
        def _():
            lsend[j] = low
            low_copy(j).start()

        @pl.when(k == n_dp)
        def _():
            lrecv[me] = low

    loop(1, n_dp + 1, low_work)

    def chain_copy():
        return remote(chain_out, chain_in, c_ss, c_rs, sec - 1, me)

    def norm_copy(q, d):
        return remote(norms.at[me], norms.at[me], n_ss.at[q, d], n_rs.at[me], q, d)

    def norm_value():
        def add(j, total):
            piece = gbuf[j]
            return total + mm_t(piece, piece)
        gram_g = lax.fori_loop(0, n_dp, add, jnp.zeros((rows, rows), jnp.float32))
        uu = mm_t(u_out[...], u_out[...])
        vv = mm_t(v_out[...], v_out[...])
        whole = jnp.sum((gram_x[...] * uu + gram_g * vv) * w2_col[...], axis=0, keepdims=True)
        return jnp.broadcast_to(jnp.sum(whole, axis=1, keepdims=True), (1, 128))

    @pl.when(sec == 0)
    def _():
        value = norm_value()
        chain_copy().wait_recv()
        norms[me] = value + chain_in[...]
        for q in range(n_sec):
            def send(d, q=q):
                @pl.when((me != d) | (q != 0))
                def _():
                    norm_copy(q, d).start()
            loop(0, n_dp, send)

    def g_third(k):
        j = 2 * near(k) + 1 - par
        w_copy(j).wait()
        acc[...] += mm_t(gbuf[j], wbuf[:, cols(j)])

    loop(0, half, g_third)

    def low_wait(j):
        @pl.when(j != me)
        def _():
            low_arrival(j).wait_recv()

    loop(0, n_dp, low_wait)
    terms = lrecv[...].reshape(n_dp * SLOT, wide)
    lane_at = lax.broadcasted_iota(jnp.int32, (rows, n_dp * SLOT), 1)
    parts = []
    for h in range(pack):
        place = jnp.where(tgt_col[...] + h * (SLOT // 2) == lane_at, 1.0, 0.0).astype(jnp.bfloat16)
        parts.append(acc[:, h * wide : (h + 1) * wide] + mm(place, terms))
    res_out[...] = (parts[0] if pack == 1 else jnp.concatenate(parts, axis=1)).astype(jnp.bfloat16)

    @pl.when(sec > 0)
    def _():
        loop(0, half, lambda k: res_copy(k).start())

    pltpu.make_async_copy(gbuf, g_out, o_sem.at[1]).start()

    @pl.when(is_top)
    def _():
        x_work()

    @pl.when(sec > 0)
    def _():
        value = norm_value()

        @pl.when(is_top)
        def _():
            chain_out[...] = value

        @pl.when(sec != top)
        def _():
            chain_copy().wait_recv()
            chain_out[...] = value + chain_in[...]
        chain_copy().start()

    def norm_wait(j):
        @pl.when((sec != 0) | (me != j))
        def _():
            remote(norms.at[j], norms.at[j], n_ss.at[0, j], n_rs.at[j], 0, partner).wait_recv()

    @pl.when(is_top)
    def _():
        loop(1, half, lambda k: og_copy(k).wait_send())

    @pl.when(sec > 0)
    def _():
        loop(0, half, lambda k: res_copy(k).wait_send())
        chain_copy().wait_send()

    loop(1, half, lambda k: x_copy(k).wait_send())
    loop(0, half, lambda k: x_forward(2 * near(k) + par).wait_send())
    loop(0, half, lambda k: g_forward(2 * near(k) + par).wait_send())

    def low_sent(j):
        @pl.when(j != me)
        def _():
            low_copy(j).wait_send()

    loop(0, n_dp, low_sent)
    pltpu.make_async_copy(xbuf, x_out, o_sem.at[0]).wait()
    pltpu.make_async_copy(gbuf, g_out, o_sem.at[1]).wait()

    loop(0, n_dp, norm_wait)
    total = jnp.maximum(jnp.sum(norms[...], axis=0), 0.0)
    fac_out[...] = jnp.minimum(1.0, limit / jnp.sqrt(total + 1e-06))

    @pl.when(sec == 0)
    def _():
        for q in range(n_sec):
            def sent(d, q=q):
                @pl.when((me != d) | (q != 0))
                def _():
                    norm_copy(q, d).wait_send()
            loop(0, n_dp, sent)


def write_kernel(x_ref, g_ref, u_ref, v_ref, fac_ref, scale_ref, down_ref, up_ref):
    scale = scale_ref[...] * fac_ref[0:1, 0:1]
    tn = (((0,), (0,)), ((), ()))
    down = lax.dot_general(u_ref[...], x_ref[0], tn, preferred_element_type=jnp.float32)
    down_ref[...] = (down * scale).astype(jnp.bfloat16)
    up = lax.dot_general(v_ref[...], g_ref[0], tn, preferred_element_type=jnp.float32)
    up_ref[...] = (up * scale).astype(jnp.bfloat16)


def per_device(n_sec, n_dp, frozen, adapt_down, adapt_up, saved_inputs, out_grad, sensor, counts):
    me = lax.axis_index("dp")
    tokens, columns = out_grad.shape[1:]
    width = columns * n_dp
    blocks = sensor.shape[1]
    block_rows = tokens // blocks
    sen_local, rank = adapt_up.shape[1:3]
    lanes = sen_local * rank
    rows = -(-tokens // 16) * 16
    pack = 2 if columns % 256 == 0 else 1
    w_rows = frozen.shape[1]

    idents = sensor[0]
    owners = idents // sen_local
    order = jnp.arange(blocks, dtype=jnp.int32)
    earlier = (owners[:, None] == owners[None, :]) & (order[:, None] < order[None, :])
    position = jnp.sum(earlier.astype(jnp.int32), axis=0)
    first = owners * SLOT + position * block_rows
    target = (first[:, None] + jnp.arange(block_rows, dtype=jnp.int32)[None, :]).reshape(-1)
    more = (0, rows - tokens)
    target = jnp.pad(target, more, constant_values=-SLOT)
    sens = jnp.pad(jnp.repeat(idents, block_rows), more, constant_values=-1)
    weights = SCALE * (NORM_TOK / counts.astype(jnp.float32))
    held = sens[:, None] == me * sen_local + jnp.arange(sen_local, dtype=jnp.int32)[None, :]
    w2 = jnp.sum(jnp.where(held, (weights * weights)[None, :], 0.0), axis=1)
    scale_col = jnp.repeat(weights, rank)[:, None]
    limit = CLIP_RMS * math.sqrt(2.0 * n_sec * n_dp * sen_local * width * rank)

    bf, f32 = jnp.bfloat16, jnp.float32
    vm = pl.BlockSpec(memory_space=pltpu.VMEM)
    anywhere = pl.BlockSpec(memory_space=pl.ANY)
    half = n_dp // 2
    dma = pltpu.SemaphoreType.DMA
    result, x_full, g_full, u, v, factor = pl.pallas_call(
        functools.partial(chain_kernel, n_sec, n_dp, rank, pack, limit),
        out_shape=(
            jax.ShapeDtypeStruct((rows, columns), bf),
            jax.ShapeDtypeStruct((n_dp, rows, columns), bf),
            jax.ShapeDtypeStruct((n_dp, rows, columns), bf),
            jax.ShapeDtypeStruct((rows, lanes), bf),
            jax.ShapeDtypeStruct((rows, lanes), bf),
            jax.ShapeDtypeStruct((1, 128), f32),
        ),
        in_specs=[anywhere] * 3 + [vm] * 6,
        out_specs=(vm, anywhere, anywhere, vm, vm, vm),
        scratch_shapes=[
            pltpu.VMEM((w_rows, width), bf),
            pltpu.VMEM((lanes, width), bf),
            pltpu.VMEM((lanes, width), bf),
            pltpu.VMEM((n_dp, rows, columns), bf),
            pltpu.VMEM((n_dp, rows, columns), bf),
            pltpu.VMEM((n_dp, SLOT, columns // pack), bf),
            pltpu.VMEM((n_dp, SLOT, columns // pack), bf),
            pltpu.VMEM((rows, columns), f32),
            pltpu.VMEM((rows, lanes), f32),
            pltpu.VMEM((rows, lanes), f32),
            pltpu.VMEM((rows, rows), f32),
            pltpu.VMEM((1, 128), f32),
            pltpu.VMEM((1, 128), f32),
            pltpu.VMEM((n_dp, 1, 128), f32),
            dma((n_dp,)),
            dma((2,)),
            dma((2,)),
            dma((n_dp,)),
            dma((half,)),
            dma((half,)),
            dma((n_dp,)),
            dma((half,)),
            dma((half,)),
            dma((half,)),
            dma((n_dp,)),
            dma((n_dp,)),
            dma,
            dma,
            dma((n_sec, n_dp)),
            dma((n_dp,)),
        ],
        compiler_params=pltpu.CompilerParams(
            collective_id=0, has_side_effects=True, vmem_limit_bytes=48 * 1024 * 1024
        ),
        name="chain",
    )(
        frozen[0],
        jnp.swapaxes(adapt_down[0], 1, 2).reshape(lanes, width),
        adapt_up[0].reshape(lanes, width),
        saved_inputs[0, 0],
        out_grad[0],
        sens[:, None],
        target[:, None],
        target[None, :],
        w2[:, None],
    )

    fixed = lambda shape: pl.BlockSpec(shape, lambda j: (0, 0))
    piece = pl.BlockSpec((1, rows, columns), lambda j: (j, 0, 0))
    grown = pl.BlockSpec((lanes, columns), lambda j: (0, j))
    down, up = pl.pallas_call(
        write_kernel,
        grid=(n_dp,),
        out_shape=(jax.ShapeDtypeStruct((lanes, width), bf),) * 2,
        in_specs=[piece, piece, fixed((rows, lanes)), fixed((rows, lanes)), fixed((1, 128)), fixed((lanes, 1))],
        out_specs=(grown, grown),
        name="write",
    )(x_full, g_full, u, v, factor, scale_col)
    return (
        result[:tokens][None, None],
        jnp.swapaxes(down.reshape(sen_local, rank, width), 1, 2)[None],
        up.reshape(sen_local, rank, width)[None],
    )


def solution(mesh):
    return jax.shard_map(
        functools.partial(per_device, mesh.shape["section"], mesh.shape["dp"]),
        mesh=mesh,
        in_specs=(
            P("section", "dp", None),
            P("section", "dp", None, None),
            P("section", "dp", None, None),
            P("section", None, None, "dp"),
            P(None, None, "dp"),
            P(),
            P("dp"),
        ),
        out_specs=(
            P("section", None, None, "dp"),
            P("section", "dp", None, None),
            P("section", "dp", None, None),
        ),
        check_vma=False,
    )
```

```python
import functools
import math

import jax
import jax.numpy as jnp
from jax import lax
from jax.experimental import pallas as pl
from jax.experimental.pallas import tpu as pltpu
from jax.sharding import PartitionSpec as P

CAP = 2
SCALE = 2.0
NORM_TOK = 1024.0
CLIP_RMS = 0.5
MESH = pl.DeviceIdType.MESH
SLOT = 16


def mm_t(a, b):
    return lax.dot_general(a, b, (((1,), (1,)), ((), ())), preferred_element_type=jnp.float32)


def mm(a, b):
    return jnp.dot(a, b, preferred_element_type=jnp.float32)


def chain_kernel(
    n_sec, n_dp, rank, pack, fold, limit,
    sensor, counts, w_hbm, dn_hbm, up_hbm, x_in, g_in,
    res_out, down_hbm, up_grad_hbm, fac_out,
    wbuf, dbuf, ubuf, xbuf, gbuf, rbuf, u_out, v_out, dprod, uprod,
    lsend, lrecv, acc, uacc, vacc, gram_x, chain_in, chain_out, norms,
    w_sem, a_sem, o_sem, x_rs, x_ss, x_fs, g_rs, og_ss, g_ss, g_fs, l_ss, l_rs, c_ss, c_rs, n_ss, n_rs,
):
    sec = lax.axis_index("section")
    me = lax.axis_index("dp")
    par = lax.rem(me, 2)
    partner = me + 1 - 2 * par
    half = n_dp // 2
    my = me // 2
    way = 1 - 2 * (my // max(half // 2, 1))
    top = n_sec - 1
    is_top = sec == top
    tokens, columns = x_in.shape
    rows = tokens
    block_rows = tokens // n_dp
    sen_local = uacc.shape[1] // rank
    wide = columns // pack
    lanes = uacc.shape[1]

    def near(k):
        return lax.rem(my + way * k + half, half)

    def cols(j):
        return pl.ds(pl.multiple_of(j * columns, columns), columns)

    def w_copy(j):
        return pltpu.make_async_copy(w_hbm.at[:, cols(j)], wbuf.at[:, cols(j)], w_sem.at[j])

    up_copy = pltpu.make_async_copy(up_hbm, ubuf, a_sem.at[0])
    dn_copy = pltpu.make_async_copy(dn_hbm, dbuf, a_sem.at[1])
    up_copy.start()
    dn_copy.start()

    def start_w(k, carry):
        w_copy(2 * near(k) + par).start()
        return carry

    def start_w_other(k, carry):
        w_copy(2 * near(k) + 1 - par).start()
        return carry

    lax.fori_loop(0, half, start_w, 0)
    lax.fori_loop(0, half, start_w_other, 0)

    barrier = pltpu.get_barrier_semaphore()
    for q in range(n_sec):
        def greet(d, carry, q=q):
            @pl.when((sec != q) | (me != d))
            def _():
                pl.semaphore_signal(barrier, inc=1, device_id=(q, d), device_id_type=MESH)
            return carry
        lax.fori_loop(0, n_dp, greet, 0)

    def folded(value):
        if fold == 1:
            return value.astype(jnp.bfloat16)
        side = columns // 2
        return jnp.concatenate([value[:, :side], value[:, side:]], axis=0).astype(jnp.bfloat16)

    def unfolded(value):
        if fold == 1:
            return value
        value = value.astype(jnp.float32)
        return jnp.concatenate([value[:rows], value[rows:]], axis=1).astype(jnp.bfloat16)

    xbuf[me] = folded(x_in[...].astype(jnp.float32))

    @pl.when(is_top)
    def _():
        gbuf[me] = folded(g_in[...].astype(jnp.float32))

    col_block = lax.broadcasted_iota(jnp.int32, (rows, 1), 0) // block_rows
    row_block = lax.broadcasted_iota(jnp.int32, (1, rows), 1) // block_rows

    def fill(b, carry):
        col, row = carry
        ident = sensor[0, b]
        return jnp.where(col_block == b, ident, col), jnp.where(row_block == b, ident, row)

    sens_col, sens_row = lax.fori_loop(
        0, n_dp, fill, (jnp.zeros((rows, 1), jnp.int32), jnp.zeros((1, rows), jnp.int32))
    )
    own_col, own_row = sens_col // sen_local, sens_row // sen_local
    col_at = lax.broadcasted_iota(jnp.int32, (rows, rows), 0)
    row_at = lax.broadcasted_iota(jnp.int32, (rows, rows), 1)
    same = own_col == own_row
    head_col = same & (col_at // block_rows < row_block) & (lax.rem(col_at, block_rows) == 0)
    head_row = same & (row_at // block_rows < col_block) & (lax.rem(row_at, block_rows) == 0)
    pos_row = jnp.sum(jnp.where(head_col, 1.0, 0.0), axis=0, keepdims=True)
    pos_col = jnp.sum(jnp.where(head_row, 1.0, 0.0), axis=1, keepdims=True)
    in_row = lax.rem(lax.broadcasted_iota(jnp.int32, (1, rows), 1), block_rows)
    in_col = lax.rem(lax.broadcasted_iota(jnp.int32, (rows, 1), 0), block_rows)
    tgt_row = own_row * SLOT + pos_row.astype(jnp.int32) * block_rows + in_row
    tgt_col = own_col * SLOT + pos_col.astype(jnp.int32) * block_rows + in_col
    w2_col = jnp.zeros((rows, 1), jnp.float32)
    for i in range(sen_local):
        weight = SCALE * NORM_TOK / jnp.full((rows, 1), counts[i], jnp.int32).astype(jnp.float32)
        w2_col = jnp.where(sens_col == me * sen_local + i, weight * weight, w2_col)
    lane_sensor = lax.broadcasted_iota(jnp.int32, (rows, lanes), 1) // rank
    own = sens_col == me * sen_local + lane_sensor

    pl.semaphore_wait(barrier, n_sec * n_dp - 1)

    def remote(src, dst, ss, rs, q, d):
        return pltpu.make_async_remote_copy(
            src_ref=src, dst_ref=dst, send_sem=ss, recv_sem=rs, device_id=(q, d), device_id_type=MESH
        )

    def og_copy(k):
        return remote(gbuf.at[me], gbuf.at[me], og_ss.at[k], g_rs.at[me], sec, 2 * near(k) + par)

    def x_copy(k):
        return remote(xbuf.at[me], xbuf.at[me], x_ss.at[k], x_rs.at[me], sec, 2 * near(k) + par)

    def x_forward(j):
        return remote(xbuf.at[j], xbuf.at[j], x_fs.at[j // 2], x_rs.at[j], sec, partner)

    def g_forward(j):
        return remote(gbuf.at[j], gbuf.at[j], g_fs.at[j // 2], g_rs.at[j], sec, partner)

    def res_copy(k):
        return remote(rbuf, gbuf.at[me], g_ss.at[k], g_rs.at[me], sec - 1, 2 * near(k) + par)

    def low_copy(j):
        return remote(lsend.at[j], lrecv.at[me], l_ss.at[j], l_rs.at[me], sec, j)

    def low_arrival(j):
        return remote(lsend.at[j], lrecv.at[j], l_ss.at[j], l_rs.at[j], sec, partner)

    def loop(lo, hi, body):
        def step(k, carry):
            body(k)
            return carry
        lax.fori_loop(lo, hi, step, 0)

    def x_work():
        loop(1, half, lambda k: x_copy(k).start())
        vacc[...] = jnp.zeros_like(vacc)
        gram_x[...] = jnp.zeros_like(gram_x)

        def use(j):
            piece = unfolded(xbuf[j])
            vacc[...] += mm_t(piece, dbuf[:, cols(j)])
            gram_x[...] += mm_t(piece, piece)

        def first(k):
            j = 2 * near(k) + par

            @pl.when(k > 0)
            def _():
                x_forward(j).wait_recv()
            x_forward(j).start()
            use(j)

        def second(k):
            j = 2 * near(k) + 1 - par
            x_forward(j).wait_recv()
            use(j)

        loop(0, half, first)
        loop(0, half, second)
        v_out[...] = jnp.where(own, vacc[...], 0.0).astype(jnp.bfloat16)

    @pl.when(is_top)
    def _():
        loop(1, half, lambda k: og_copy(k).start())

    dn_copy.wait()
    up_copy.wait()

    @pl.when(sec != top)
    def _():
        x_work()

    acc[...] = jnp.zeros_like(acc)
    uacc[...] = jnp.zeros_like(uacc)

    def g_first(k):
        j = 2 * near(k) + par

        @pl.when((k > 0) | (sec != top))
        def _():
            g_forward(j).wait_recv()
        g_forward(j).start()
        w_copy(j).wait()
        piece = unfolded(gbuf[j])
        uacc[...] += mm_t(piece, ubuf[:, cols(j)])
        acc[...] += mm_t(piece, wbuf[:, cols(j)])

    def g_second(k):
        j = 2 * near(k) + 1 - par
        g_forward(j).wait_recv()
        uacc[...] += mm_t(unfolded(gbuf[j]), ubuf[:, cols(j)])

    loop(0, half, g_first)
    loop(0, half, g_second)
    u_out[...] = jnp.where(own, uacc[...], 0.0).astype(jnp.bfloat16)

    slot_at = lax.broadcasted_iota(jnp.int32, (SLOT, rows), 0) + me * SLOT
    in_slot = lax.broadcasted_iota(jnp.int32, (SLOT, rows), 0) < SLOT // pack
    select = jnp.where((tgt_row == slot_at) & in_slot, 1.0, 0.0).astype(jnp.bfloat16)
    u_sel = mm(select, u_out[...]).astype(jnp.bfloat16)

    def low_work(k):
        j = lax.rem(me + k, n_dp)
        low = SCALE * mm(u_sel, dbuf[:, cols(j)])
        if pack == 2:
            low = jnp.concatenate([low[: SLOT // 2, :wide], low[: SLOT // 2, wide:]], axis=0)
        low = low.astype(jnp.bfloat16)

        @pl.when(k < n_dp)
        def _():
            lsend[j] = low
            low_copy(j).start()

        @pl.when(k == n_dp)
        def _():
            lrecv[me] = low

    loop(1, n_dp + 1, low_work)

    def chain_copy():
        return remote(chain_out, chain_in, c_ss, c_rs, sec - 1, me)

    def norm_copy(q, d):
        return remote(norms.at[me], norms.at[me], n_ss.at[q, d], n_rs.at[me], q, d)

    def norm_value():
        def add(j, total):
            piece = unfolded(gbuf[j])
            return total + mm_t(piece, piece)
        gram_g = lax.fori_loop(0, n_dp, add, jnp.zeros((rows, rows), jnp.float32))
        uu = mm_t(u_out[...], u_out[...])
        vv = mm_t(v_out[...], v_out[...])
        whole = jnp.sum((gram_x[...] * uu + gram_g * vv) * w2_col, axis=0, keepdims=True)
        return jnp.broadcast_to(jnp.sum(whole, axis=1, keepdims=True), (1, 128))

    @pl.when(sec == 0)
    def _():
        value = norm_value()
        chain_copy().wait_recv()
        norms[me] = value + chain_in[...]
        for q in range(n_sec):
            def send(d, q=q):
                @pl.when((me != d) | (q != 0))
                def _():
                    norm_copy(q, d).start()
            loop(0, n_dp, send)

    def g_third(k):
        j = 2 * near(k) + 1 - par
        w_copy(j).wait()
        acc[...] += mm_t(unfolded(gbuf[j]), wbuf[:, cols(j)])

    loop(0, half, g_third)

    def low_wait(j):
        @pl.when(j != me)
        def _():
            low_arrival(j).wait_recv()

    loop(0, n_dp, low_wait)
    terms = lrecv[...].reshape(n_dp * SLOT, wide)
    lane_at = lax.broadcasted_iota(jnp.int32, (rows, n_dp * SLOT), 1)
    parts = []
    for h in range(pack):
        place = jnp.where(tgt_col + h * (SLOT // 2) == lane_at, 1.0, 0.0).astype(jnp.bfloat16)
        parts.append(acc[:, h * wide : (h + 1) * wide] + mm(place, terms))
    result = parts[0] if pack == 1 else jnp.concatenate(parts, axis=1)
    rbuf[...] = folded(result)

    @pl.when(sec > 0)
    def _():
        loop(0, half, lambda k: res_copy(k).start())

    res_out[...] = result.astype(jnp.bfloat16)

    @pl.when(is_top)
    def _():
        x_work()

    @pl.when(sec > 0)
    def _():
        value = norm_value()

        @pl.when(is_top)
        def _():
            chain_out[...] = value

        @pl.when(sec != top)
        def _():
            chain_copy().wait_recv()
            chain_out[...] = value + chain_in[...]
        chain_copy().start()

    def down_copy(j):
        return pltpu.make_async_copy(dprod.at[:, cols(j)], down_hbm.at[:, cols(j)], o_sem.at[0, j])

    def up_grad_copy(j):
        return pltpu.make_async_copy(uprod.at[:, cols(j)], up_grad_hbm.at[:, cols(j)], o_sem.at[1, j])

    u_t = u_out[...].astype(jnp.float32).T.astype(jnp.bfloat16)
    v_t = v_out[...].astype(jnp.float32).T.astype(jnp.bfloat16)

    def grow(j):
        dprod[:, cols(j)] = mm(u_t, unfolded(xbuf[j])).astype(jnp.bfloat16)
        down_copy(j).start()
        uprod[:, cols(j)] = mm(v_t, unfolded(gbuf[j])).astype(jnp.bfloat16)
        up_grad_copy(j).start()

    loop(0, n_dp, grow)

    def norm_wait(j):
        @pl.when((sec != 0) | (me != j))
        def _():
            remote(norms.at[j], norms.at[j], n_ss.at[0, j], n_rs.at[j], 0, partner).wait_recv()

    @pl.when(is_top)
    def _():
        loop(1, half, lambda k: og_copy(k).wait_send())

    @pl.when(sec > 0)
    def _():
        loop(0, half, lambda k: res_copy(k).wait_send())
        chain_copy().wait_send()

    loop(1, half, lambda k: x_copy(k).wait_send())
    loop(0, half, lambda k: x_forward(2 * near(k) + par).wait_send())
    loop(0, half, lambda k: g_forward(2 * near(k) + par).wait_send())

    def low_sent(j):
        @pl.when(j != me)
        def _():
            low_copy(j).wait_send()

    loop(0, n_dp, low_sent)
    loop(0, n_dp, lambda j: down_copy(j).wait())
    loop(0, n_dp, lambda j: up_grad_copy(j).wait())

    loop(0, n_dp, norm_wait)
    total = jnp.maximum(jnp.sum(norms[...], axis=0), 0.0)
    fac_out[...] = jnp.minimum(1.0, limit / jnp.sqrt(total + 1e-06))

    @pl.when(sec == 0)
    def _():
        for q in range(n_sec):
            def sent(d, q=q):
                @pl.when((me != d) | (q != 0))
                def _():
                    norm_copy(q, d).wait_send()
            loop(0, n_dp, sent)


def per_device(n_sec, n_dp, frozen, adapt_down, adapt_up, saved_inputs, out_grad, sensor, counts):
    tokens, columns = out_grad.shape[1:]
    width = columns * n_dp
    sen_local, rank = adapt_up.shape[1:3]
    lanes = sen_local * rank
    pack = 2 if columns % 256 == 0 else 1
    fold = 2 if tokens % 16 else 1
    rows = tokens
    w_rows = frozen.shape[1]
    limit = CLIP_RMS * math.sqrt(2.0 * n_sec * n_dp * sen_local * width * rank)

    bf, f32 = jnp.bfloat16, jnp.float32
    vm = pl.BlockSpec(memory_space=pltpu.VMEM)
    anywhere = pl.BlockSpec(memory_space=pl.ANY)
    half = n_dp // 2
    dma = pltpu.SemaphoreType.DMA
    smem = pl.BlockSpec(memory_space=pltpu.SMEM)
    result, down, up, factor = pl.pallas_call(
        functools.partial(chain_kernel, n_sec, n_dp, rank, pack, fold, limit),
        out_shape=(
            jax.ShapeDtypeStruct((rows, columns), bf),
            jax.ShapeDtypeStruct((lanes, width), bf),
            jax.ShapeDtypeStruct((lanes, width), bf),
            jax.ShapeDtypeStruct((1, 128), f32),
        ),
        in_specs=[smem] * 2 + [anywhere] * 3 + [vm] * 2,
        out_specs=(vm, anywhere, anywhere, vm),
        scratch_shapes=[
            pltpu.VMEM((w_rows, width), bf),
            pltpu.VMEM((lanes, width), bf),
            pltpu.VMEM((lanes, width), bf),
            pltpu.VMEM((n_dp, rows * fold, columns // fold), bf),
            pltpu.VMEM((n_dp, rows * fold, columns // fold), bf),
            pltpu.VMEM((rows * fold, columns // fold), bf),
            pltpu.VMEM((rows, lanes), bf),
            pltpu.VMEM((rows, lanes), bf),
            pltpu.VMEM((lanes, width), bf),
            pltpu.VMEM((lanes, width), bf),
            pltpu.VMEM((n_dp, SLOT, columns // pack), bf),
            pltpu.VMEM((n_dp, SLOT, columns // pack), bf),
            pltpu.VMEM((rows, columns), f32),
            pltpu.VMEM((rows, lanes), f32),
            pltpu.VMEM((rows, lanes), f32),
            pltpu.VMEM((rows, rows), f32),
            pltpu.VMEM((1, 128), f32),
            pltpu.VMEM((1, 128), f32),
            pltpu.VMEM((n_dp, 1, 128), f32),
            dma((n_dp,)),
            dma((2,)),
            dma((2, n_dp)),
            dma((n_dp,)),
            dma((half,)),
            dma((half,)),
            dma((n_dp,)),
            dma((half,)),
            dma((half,)),
            dma((half,)),
            dma((n_dp,)),
            dma((n_dp,)),
            dma,
            dma,
            dma((n_sec, n_dp)),
            dma((n_dp,)),
        ],
        compiler_params=pltpu.CompilerParams(
            collective_id=0, has_side_effects=True, vmem_limit_bytes=60 * 1024 * 1024
        ),
        name="chain",
    )(
        sensor,
        counts,
        frozen[0],
        jnp.swapaxes(adapt_down[0], 1, 2).reshape(lanes, width),
        adapt_up[0].reshape(lanes, width),
        saved_inputs[0, 0],
        out_grad[0],
    )
    scale = (SCALE * NORM_TOK / counts.astype(f32) * factor[0, 0])[:, None, None]
    down = (down.reshape(sen_local, rank, width) * scale).astype(bf)
    up = (up.reshape(sen_local, rank, width) * scale).astype(bf)
    return result[None, None], jnp.swapaxes(down, 1, 2)[None], up[None]


def solution(mesh):
    return jax.shard_map(
        functools.partial(per_device, mesh.shape["section"], mesh.shape["dp"]),
        mesh=mesh,
        in_specs=(
            P("section", "dp", None),
            P("section", "dp", None, None),
            P("section", "dp", None, None),
            P("section", None, None, "dp"),
            P(None, None, "dp"),
            P(),
            P("dp"),
        ),
        out_specs=(
            P("section", None, None, "dp"),
            P("section", "dp", None, None),
            P("section", "dp", None, None),
        ),
        check_vma=False,
    )
```

```python
import functools
import math

import jax
import jax.numpy as jnp
from jax import lax
from jax.experimental import pallas as pl
from jax.experimental.pallas import tpu as pltpu
from jax.sharding import PartitionSpec as P

CAP = 2
SCALE = 2.0
NORM_TOK = 1024.0
CLIP_RMS = 0.5
MESH = pl.DeviceIdType.MESH
SLOT = 16


def mm_t(a, b):
    return lax.dot_general(a, b, (((1,), (1,)), ((), ())), preferred_element_type=jnp.float32)


def mm(a, b):
    return jnp.dot(a, b, preferred_element_type=jnp.float32)


def chain_kernel(
    n_sec, n_dp, rank, pack, fold, limit,
    sensor, counts, w_hbm, dn_hbm, up_hbm, x_in, g_in,
    res_out, down_hbm, up_grad_hbm, fac_out,
    wbuf, dbuf, ubuf, xbuf, gbuf, rbuf, u_out, v_out, dprod, uprod,
    lsend, lrecv, acc, uacc, vacc, gram_x, chain_in, chain_out, norms, total_in,
    w_sem, a_sem, o_sem, x_rs, x_ss, x_fs, g_rs, og_ss, g_ss, g_fs, l_ss, l_rs, c_ss, c_rs, n_ss, n_rs, t_ss, t_rs,
):
    sec = lax.axis_index("section")
    me = lax.axis_index("dp")
    par = lax.rem(me, 2)
    partner = me + 1 - 2 * par
    half = n_dp // 2
    my = me // 2
    way = 1 - 2 * (my // max(half // 2, 1))
    top = n_sec - 1
    is_top = sec == top
    tokens, columns = x_in.shape
    rows = tokens
    block_rows = tokens // n_dp
    sen_local = uacc.shape[1] // rank
    wide = columns // pack
    lanes = uacc.shape[1]

    def near(k):
        return lax.rem(my + way * k + half, half)

    def cols(j):
        return pl.ds(pl.multiple_of(j * columns, columns), columns)

    def w_copy(j):
        return pltpu.make_async_copy(w_hbm.at[:, cols(j)], wbuf.at[:, cols(j)], w_sem.at[j])

    up_copy = pltpu.make_async_copy(up_hbm, ubuf, a_sem.at[0])
    dn_copy = pltpu.make_async_copy(dn_hbm, dbuf, a_sem.at[1])
    up_copy.start()
    dn_copy.start()

    def start_w(k, carry):
        w_copy(2 * near(k) + par).start()
        return carry

    def start_w_other(k, carry):
        w_copy(2 * near(k) + 1 - par).start()
        return carry

    lax.fori_loop(0, half, start_w, 0)
    lax.fori_loop(0, half, start_w_other, 0)

    barrier = pltpu.get_barrier_semaphore()
    def greet(q, d):
        pl.semaphore_signal(barrier, inc=1, device_id=(q, d), device_id_type=MESH)

    def greet_own(k, carry):
        greet(sec, lax.rem(me + k, n_dp))
        return carry

    def greet_below(k, carry):
        greet(sec - 1, 2 * near(k) + par)
        return carry

    def greet_above(k, carry):
        greet(sec + 1, 2 * near(k) + par)
        return carry

    lax.fori_loop(1, n_dp, greet_own, 0)

    @pl.when(sec > 0)
    def _():
        lax.fori_loop(0, half, greet_below, 0)

    @pl.when(sec < top)
    def _():
        lax.fori_loop(0, half, greet_above, 0)

    @pl.when(sec == 0)
    def _():
        for q in range(2, n_sec):
            greet(q, me)

    @pl.when(sec > 1)
    def _():
        greet(0, me)

    greeted = n_dp - 1 + jnp.where(sec > 0, half, 0) + jnp.where(sec < top, half, 0)
    greeted = greeted + jnp.where(sec == 0, n_sec - 2, jnp.where(sec > 1, 1, 0))

    def folded(value):
        if fold == 1:
            return value.astype(jnp.bfloat16)
        side = columns // 2
        return jnp.concatenate([value[:, :side], value[:, side:]], axis=0).astype(jnp.bfloat16)

    def unfolded(value):
        if fold == 1:
            return value
        value = value.astype(jnp.float32)
        return jnp.concatenate([value[:rows], value[rows:]], axis=1).astype(jnp.bfloat16)

    xbuf[me] = folded(x_in[...].astype(jnp.float32))

    @pl.when(is_top)
    def _():
        gbuf[me] = folded(g_in[...].astype(jnp.float32))

    col_block = lax.broadcasted_iota(jnp.int32, (rows, 1), 0) // block_rows
    row_block = lax.broadcasted_iota(jnp.int32, (1, rows), 1) // block_rows

    def fill(b, carry):
        col, row = carry
        ident = sensor[0, b]
        return jnp.where(col_block == b, ident, col), jnp.where(row_block == b, ident, row)

    sens_col, sens_row = lax.fori_loop(
        0, n_dp, fill, (jnp.zeros((rows, 1), jnp.int32), jnp.zeros((1, rows), jnp.int32))
    )
    own_col, own_row = sens_col // sen_local, sens_row // sen_local
    col_at = lax.broadcasted_iota(jnp.int32, (rows, rows), 0)
    row_at = lax.broadcasted_iota(jnp.int32, (rows, rows), 1)
    same = own_col == own_row
    head_col = same & (col_at // block_rows < row_block) & (lax.rem(col_at, block_rows) == 0)
    head_row = same & (row_at // block_rows < col_block) & (lax.rem(row_at, block_rows) == 0)
    pos_row = jnp.sum(jnp.where(head_col, 1.0, 0.0), axis=0, keepdims=True)
    pos_col = jnp.sum(jnp.where(head_row, 1.0, 0.0), axis=1, keepdims=True)
    in_row = lax.rem(lax.broadcasted_iota(jnp.int32, (1, rows), 1), block_rows)
    in_col = lax.rem(lax.broadcasted_iota(jnp.int32, (rows, 1), 0), block_rows)
    tgt_row = own_row * SLOT + pos_row.astype(jnp.int32) * block_rows + in_row
    tgt_col = own_col * SLOT + pos_col.astype(jnp.int32) * block_rows + in_col
    w2_col = jnp.zeros((rows, 1), jnp.float32)
    for i in range(sen_local):
        weight = SCALE * NORM_TOK / jnp.full((rows, 1), counts[i], jnp.int32).astype(jnp.float32)
        w2_col = jnp.where(sens_col == me * sen_local + i, weight * weight, w2_col)
    lane_sensor = lax.broadcasted_iota(jnp.int32, (rows, lanes), 1) // rank
    own = sens_col == me * sen_local + lane_sensor

    pl.semaphore_wait(barrier, greeted)

    def remote(src, dst, ss, rs, q, d):
        return pltpu.make_async_remote_copy(
            src_ref=src, dst_ref=dst, send_sem=ss, recv_sem=rs, device_id=(q, d), device_id_type=MESH
        )

    def og_copy(k):
        return remote(gbuf.at[me], gbuf.at[me], og_ss.at[k], g_rs.at[me], sec, 2 * near(k) + par)

    def x_copy(k):
        return remote(xbuf.at[me], xbuf.at[me], x_ss.at[k], x_rs.at[me], sec, 2 * near(k) + par)

    def x_forward(j):
        return remote(xbuf.at[j], xbuf.at[j], x_fs.at[j // 2], x_rs.at[j], sec, partner)

    def g_forward(j):
        return remote(gbuf.at[j], gbuf.at[j], g_fs.at[j // 2], g_rs.at[j], sec, partner)

    def res_copy(k):
        return remote(rbuf, gbuf.at[me], g_ss.at[k], g_rs.at[me], sec - 1, 2 * near(k) + par)

    def low_copy(j):
        return remote(lsend.at[j], lrecv.at[me], l_ss.at[j], l_rs.at[me], sec, j)

    def low_arrival(j):
        return remote(lsend.at[j], lrecv.at[j], l_ss.at[j], l_rs.at[j], sec, partner)

    def loop(lo, hi, body):
        def step(k, carry):
            body(k)
            return carry
        lax.fori_loop(lo, hi, step, 0)

    def loop_flat(lo, hi, body):
        if hi - lo > 8:
            loop(lo, hi, body)
        else:
            for k in range(lo, hi):
                body(k)

    def x_work():
        loop(1, half, lambda k: x_copy(k).start())
        vacc[...] = jnp.zeros_like(vacc)
        gram_x[...] = jnp.zeros_like(gram_x)

        def use(j):
            piece = unfolded(xbuf[j])
            vacc[...] += mm_t(piece, dbuf[:, cols(j)])
            gram_x[...] += mm_t(piece, piece)

        def first(k):
            j = 2 * near(k) + par

            @pl.when(k > 0)
            def _():
                x_forward(j).wait_recv()
            x_forward(j).start()
            use(j)

        def second(k):
            j = 2 * near(k) + 1 - par
            x_forward(j).wait_recv()
            use(j)

        loop(0, half, first)
        loop(0, half, second)
        v_out[...] = jnp.where(own, vacc[...], 0.0).astype(jnp.bfloat16)

    @pl.when(is_top)
    def _():
        loop(1, half, lambda k: og_copy(k).start())

    dn_copy.wait()
    up_copy.wait()

    @pl.when(sec != top)
    def _():
        x_work()

    acc[...] = jnp.zeros_like(acc)
    uacc[...] = jnp.zeros_like(uacc)

    def g_first(k):
        j = 2 * near(k) + par

        @pl.when((k > 0) | (sec != top))
        def _():
            g_forward(j).wait_recv()
        g_forward(j).start()
        w_copy(j).wait()
        piece = unfolded(gbuf[j])
        uacc[...] += mm_t(piece, ubuf[:, cols(j)])
        acc[...] += mm_t(piece, wbuf[:, cols(j)])

    def g_second(k):
        j = 2 * near(k) + 1 - par
        g_forward(j).wait_recv()
        uacc[...] += mm_t(unfolded(gbuf[j]), ubuf[:, cols(j)])

    loop(0, half, g_first)
    loop_flat(0, half, g_second)
    u_out[...] = jnp.where(own, uacc[...], 0.0).astype(jnp.bfloat16)

    slot_at = lax.broadcasted_iota(jnp.int32, (SLOT, rows), 0) + me * SLOT
    in_slot = lax.broadcasted_iota(jnp.int32, (SLOT, rows), 0) < SLOT // pack
    select = jnp.where((tgt_row == slot_at) & in_slot, 1.0, 0.0).astype(jnp.bfloat16)
    u_sel = mm(select, u_out[...]).astype(jnp.bfloat16)

    def low_of(j):
        low = SCALE * mm(u_sel, dbuf[:, cols(j)])
        if pack == 2:
            low = jnp.concatenate([low[: SLOT // 2, :wide], low[: SLOT // 2, wide:]], axis=0)
        return low.astype(jnp.bfloat16)

    def low_work(k):
        j = lax.rem(me + k, n_dp)
        lsend[j] = low_of(j)
        low_copy(j).start()

    loop_flat(1, n_dp, low_work)
    lrecv[me] = low_of(me)

    def chain_copy():
        return remote(chain_out, chain_in, c_ss, c_rs, sec - 1, me)

    def norm_copy(d):
        return remote(norms.at[me], norms.at[me], n_ss.at[d], n_rs.at[me], 0, d)

    def total_copy(q):
        return remote(total_in, total_in, t_ss.at[q], t_rs, q, me)

    def norm_value():
        def add(j, total):
            piece = unfolded(gbuf[j])
            return total + mm_t(piece, piece)
        gram_g = lax.fori_loop(0, n_dp, add, jnp.zeros((rows, rows), jnp.float32))
        uu = mm_t(u_out[...], u_out[...])
        vv = mm_t(v_out[...], v_out[...])
        whole = jnp.sum((gram_x[...] * uu + gram_g * vv) * w2_col, axis=0, keepdims=True)
        return jnp.broadcast_to(jnp.sum(whole, axis=1, keepdims=True), (1, 128))

    @pl.when(sec == 0)
    def _():
        value = norm_value()
        chain_copy().wait_recv()
        norms[me] = value + chain_in[...]
        loop(1, n_dp, lambda k: norm_copy(lax.rem(me + k, n_dp)).start())

    def g_third(k):
        j = 2 * near(k) + 1 - par
        w_copy(j).wait()
        acc[...] += mm_t(unfolded(gbuf[j]), wbuf[:, cols(j)])

    loop_flat(0, half, g_third)

    def norm_wait(k):
        j = lax.rem(me + k, n_dp)
        remote(norms.at[j], norms.at[j], n_ss.at[j], n_rs.at[j], 0, partner).wait_recv()

    @pl.when(sec == 0)
    def _():
        loop(1, n_dp, norm_wait)
        total_in[...] = jnp.sum(norms[...], axis=0)
        for q in range(1, n_sec):
            total_copy(q).start()

    def low_wait(j):
        @pl.when(j != me)
        def _():
            low_arrival(j).wait_recv()

    loop(0, n_dp, low_wait)
    terms = lrecv[...].reshape(n_dp * SLOT, wide)
    lane_at = lax.broadcasted_iota(jnp.int32, (rows, n_dp * SLOT), 1)
    parts = []
    for h in range(pack):
        place = jnp.where(tgt_col + h * (SLOT // 2) == lane_at, 1.0, 0.0).astype(jnp.bfloat16)
        parts.append(acc[:, h * wide : (h + 1) * wide] + mm(place, terms))
    result = parts[0] if pack == 1 else jnp.concatenate(parts, axis=1)
    rbuf[...] = folded(result)

    @pl.when(sec > 0)
    def _():
        loop(0, half, lambda k: res_copy(k).start())

    res_out[...] = result.astype(jnp.bfloat16)

    @pl.when(is_top)
    def _():
        x_work()

    @pl.when(sec > 0)
    def _():
        value = norm_value()

        @pl.when(is_top)
        def _():
            chain_out[...] = value

        @pl.when(sec != top)
        def _():
            chain_copy().wait_recv()
            chain_out[...] = value + chain_in[...]
        chain_copy().start()

    def down_copy(j):
        return pltpu.make_async_copy(dprod.at[:, cols(j)], down_hbm.at[:, cols(j)], o_sem.at[0, j])

    def up_grad_copy(j):
        return pltpu.make_async_copy(uprod.at[:, cols(j)], up_grad_hbm.at[:, cols(j)], o_sem.at[1, j])

    u_t = u_out[...].astype(jnp.float32).T.astype(jnp.bfloat16)
    v_t = v_out[...].astype(jnp.float32).T.astype(jnp.bfloat16)

    def grow(j):
        dprod[:, cols(j)] = mm(u_t, unfolded(xbuf[j])).astype(jnp.bfloat16)
        down_copy(j).start()
        uprod[:, cols(j)] = mm(v_t, unfolded(gbuf[j])).astype(jnp.bfloat16)
        up_grad_copy(j).start()

    loop(0, n_dp, grow)

    @pl.when(is_top)
    def _():
        loop(1, half, lambda k: og_copy(k).wait_send())

    @pl.when(sec > 0)
    def _():
        loop(0, half, lambda k: res_copy(k).wait_send())
        chain_copy().wait_send()

    loop(1, half, lambda k: x_copy(k).wait_send())
    loop(0, half, lambda k: x_forward(2 * near(k) + par).wait_send())
    loop(0, half, lambda k: g_forward(2 * near(k) + par).wait_send())

    def low_sent(j):
        @pl.when(j != me)
        def _():
            low_copy(j).wait_send()

    loop(0, n_dp, low_sent)
    loop(0, n_dp, lambda j: down_copy(j).wait())
    loop(0, n_dp, lambda j: up_grad_copy(j).wait())

    @pl.when(sec > 0)
    def _():
        total_copy(0).wait_recv()

    total = jnp.maximum(total_in[...], 0.0)
    fac_out[...] = jnp.minimum(1.0, limit / jnp.sqrt(total + 1e-06))

    @pl.when(sec == 0)
    def _():
        loop(1, n_dp, lambda k: norm_copy(lax.rem(me + k, n_dp)).wait_send())
        for q in range(1, n_sec):
            total_copy(q).wait_send()


def per_device(n_sec, n_dp, frozen, adapt_down, adapt_up, saved_inputs, out_grad, sensor, counts):
    tokens, columns = out_grad.shape[1:]
    width = columns * n_dp
    sen_local, rank = adapt_up.shape[1:3]
    lanes = sen_local * rank
    pack = 2 if columns % 256 == 0 else 1
    fold = 2 if tokens % 16 else 1
    rows = tokens
    w_rows = frozen.shape[1]
    limit = CLIP_RMS * math.sqrt(2.0 * n_sec * n_dp * sen_local * width * rank)

    bf, f32 = jnp.bfloat16, jnp.float32
    vm = pl.BlockSpec(memory_space=pltpu.VMEM)
    anywhere = pl.BlockSpec(memory_space=pl.ANY)
    half = n_dp // 2
    dma = pltpu.SemaphoreType.DMA
    smem = pl.BlockSpec(memory_space=pltpu.SMEM)
    result, down, up, factor = pl.pallas_call(
        functools.partial(chain_kernel, n_sec, n_dp, rank, pack, fold, limit),
        out_shape=(
            jax.ShapeDtypeStruct((rows, columns), bf),
            jax.ShapeDtypeStruct((lanes, width), bf),
            jax.ShapeDtypeStruct((lanes, width), bf),
            jax.ShapeDtypeStruct((1, 128), f32),
        ),
        in_specs=[smem] * 2 + [anywhere] * 3 + [vm] * 2,
        out_specs=(vm, anywhere, anywhere, vm),
        scratch_shapes=[
            pltpu.VMEM((w_rows, width), bf),
            pltpu.VMEM((lanes, width), bf),
            pltpu.VMEM((lanes, width), bf),
            pltpu.VMEM((n_dp, rows * fold, columns // fold), bf),
            pltpu.VMEM((n_dp, rows * fold, columns // fold), bf),
            pltpu.VMEM((rows * fold, columns // fold), bf),
            pltpu.VMEM((rows, lanes), bf),
            pltpu.VMEM((rows, lanes), bf),
            pltpu.VMEM((lanes, width), bf),
            pltpu.VMEM((lanes, width), bf),
            pltpu.VMEM((n_dp, SLOT, columns // pack), bf),
            pltpu.VMEM((n_dp, SLOT, columns // pack), bf),
            pltpu.VMEM((rows, columns), f32),
            pltpu.VMEM((rows, lanes), f32),
            pltpu.VMEM((rows, lanes), f32),
            pltpu.VMEM((rows, rows), f32),
            pltpu.VMEM((1, 128), f32),
            pltpu.VMEM((1, 128), f32),
            pltpu.VMEM((n_dp, 1, 128), f32),
            pltpu.VMEM((1, 128), f32),
            dma((n_dp,)),
            dma((2,)),
            dma((2, n_dp)),
            dma((n_dp,)),
            dma((half,)),
            dma((half,)),
            dma((n_dp,)),
            dma((half,)),
            dma((half,)),
            dma((half,)),
            dma((n_dp,)),
            dma((n_dp,)),
            dma,
            dma,
            dma((n_dp,)),
            dma((n_dp,)),
            dma((n_sec,)),
            dma,
        ],
        compiler_params=pltpu.CompilerParams(
            collective_id=0, has_side_effects=True, vmem_limit_bytes=60 * 1024 * 1024
        ),
        name="chain",
    )(
        sensor,
        counts,
        frozen[0],
        jnp.swapaxes(adapt_down[0], 1, 2).reshape(lanes, width),
        adapt_up[0].reshape(lanes, width),
        saved_inputs[0, 0],
        out_grad[0],
    )
    scale = (SCALE * NORM_TOK / counts.astype(f32) * factor[0, 0])[:, None, None]
    down = (down.reshape(sen_local, rank, width) * scale).astype(bf)
    up = (up.reshape(sen_local, rank, width) * scale).astype(bf)
    return result[None, None], jnp.swapaxes(down, 1, 2)[None], up[None]


def solution(mesh):
    return jax.shard_map(
        functools.partial(per_device, mesh.shape["section"], mesh.shape["dp"]),
        mesh=mesh,
        in_specs=(
            P("section", "dp", None),
            P("section", "dp", None, None),
            P("section", "dp", None, None),
            P("section", None, None, "dp"),
            P(None, None, "dp"),
            P(),
            P("dp"),
        ),
        out_specs=(
            P("section", None, None, "dp"),
            P("section", "dp", None, None),
            P("section", "dp", None, None),
        ),
        check_vma=False,
    )
```
